128 devices in a mesh: rows: 32 (over y, x_lo, z), cols: 4 (over x_hi, core).
Axes of the slice: x: 4 (x_hi: 2, x_lo: 2; x = x_hi * 2 + x_lo), y: 4, z: 4, core: 2. Of those that a mesh axis runs over, the one named last changes fastest.
Arguments:
- local_tiles: bfloat16 [1024, 24, 64, 64], P('rows'), may hold values from -0.109375 to 0.109375
- local_cols: int32 [1024, 24], P('rows'), may hold values from 0 to 31, as said below
- section_tiles: bfloat16 [1024, 2, 12, 64, 64], P('rows'), may hold values from -0.109375 to 0.109375
- section_cols: int32 [1024, 2, 12], P('rows'), may hold values from 0 to 31, as said below
- owners: int32 [2], replicated, may hold values from 0 to 31
- prol_tiles: bfloat16 [1024, 8, 64, 64], P('rows', 'cols'), may hold values from -6 to 6
- prol_cols: int32 [1024, 8], P('rows', 'cols'), may hold values from 0 to 7, as said below
Outputs:
- product: bfloat16 [65536, 2048], P('rows')
The draws below stay inside these ranges and needn't reach their ends.
Inputs may be any that keep to these rules, and one draw needn't show every extreme that they name: `local_cols`: the 24 entries of one block row are distinct. `section_cols`: the 12 entries of one block row and section are distinct. `prol_cols`: within one block row, the 2 entries of each index of cols are distinct.
All inputs are finite; a program needn't handle non-finite values.
Results may differ from the reference program's by a relative error of at most 0.001.
Values may be sent and summed in bfloat16 or wider, within the bound.
A program may use at most 256 MiB of HBM per device.

```python
import jax
import jax.numpy as jnp
from jax import lax

B = 64
RB = 32
K = 24
KS = 12
SECTIONS = 2
CTD = 8
KPD = 2
KP = 8
NB = 1024
NC = 2048
N_ROWS = 32


def distinct_rows(key, count, pool, take):
    keys = jax.random.split(key, count)
    return jax.vmap(lambda single: jax.random.permutation(single, pool)[:take])(keys).astype(jnp.int32)


def draw_local_cols(key, part):
    key = jax.random.fold_in(key, 11)
    return distinct_rows(key, NB, RB, K)


def draw_section_cols(key, part):
    key = jax.random.fold_in(key, 23)
    return distinct_rows(key, NB * SECTIONS, RB, KS).reshape(NB, SECTIONS, KS)


def draw_prol_cols(key, part):
    key = jax.random.fold_in(key, 37)
    return distinct_rows(key, NB * (KP // KPD), CTD, KPD).reshape(NB, KP)


def steps_of(own_key, dims, cuts, smallest, top_value):
    loudness, own = 1.0, jax.random.fold_in(own_key, 6)
    for dim, shards_of in cuts:
        steps = jnp.exp(jax.random.uniform(jax.random.fold_in(own, dim), (shards_of,), jnp.float32, smallest / len(cuts), top_value / len(cuts)))
        loudness = loudness * jnp.repeat(steps, dims[dim] // shards_of).reshape([-1 if axis == dim else 1 for axis in range(len(dims))])
    return loudness


def noise(rng, extent, deviation, reach, pieces=(), held_as=jnp.bfloat16):
    factor_of = steps_of(rng, extent, pieces, -0.22, 0.18) if pieces else 1.0
    values = jax.random.normal(rng, extent, jnp.float32) * deviation * factor_of
    return jnp.minimum(jnp.maximum(values, -reach), reach).astype(held_as)


def setup_inputs(seed: int = 0) -> dict:
    key_of = jax.random.split(jax.random.key(seed), 8)
    return {
        "local_tiles": noise(key_of[0], (NB, K, B, B), (B * (K + SECTIONS * KS)) ** -0.5, 0.109375, ((0, 32),)),
        "local_cols": draw_local_cols(jax.random.fold_in(key_of[7], 71), 0),
        "section_tiles": noise(key_of[2], (NB, SECTIONS, KS, B, B), (B * (K + SECTIONS * KS)) ** -0.5, 0.109375, ((0, 32),)),
        "section_cols": draw_section_cols(jax.random.fold_in(key_of[7], 71), 0),
        "owners": jax.random.randint(key_of[4], (SECTIONS,), 0, N_ROWS).astype(jnp.int32),
        "prol_tiles": noise(key_of[5], (NB, KP, B, B), 1.0, 6.0, ((0, 32), (1, 4))),
        "prol_cols": draw_prol_cols(jax.random.fold_in(key_of[7], 71), 0),
    }


def reference(local_tiles, local_cols, section_tiles, section_cols, owners, prol_tiles, prol_cols):
    tile_total = NC // B
    offsets = ((jnp.arange(KP) // KPD) * CTD).astype(jnp.int32)

    def dense_row(index):
        target = (offsets + prol_cols[index]).astype(jnp.int32)
        onehot = (target[:, None] == jnp.arange(tile_total, dtype=jnp.int32)[None, :]).astype(jnp.float32)
        row = jnp.einsum("jt,jab->atb", onehot, prol_tiles[index].astype(jnp.float32))
        return row.reshape(B, NC).astype(jnp.bfloat16)

    blocks = lax.map(dense_row, jnp.arange(NB, dtype=jnp.int32))
    groups = (jnp.arange(NB) // RB).astype(jnp.int32)

    def one_row(index):
        own = (groups[index] * RB + local_cols[index]).astype(jnp.int32)
        picked = blocks[own].astype(jnp.float32)
        total = jnp.einsum("kab,kbc->ac", local_tiles[index].astype(jnp.float32), picked)
        far = (owners[:, None] * RB + section_cols[index]).astype(jnp.int32)
        remote = blocks[far].astype(jnp.float32)
        total = total + jnp.einsum("skab,skbc->ac", section_tiles[index].astype(jnp.float32), remote)
        return total.astype(jnp.bfloat16)

    result = lax.map(one_row, jnp.arange(NB, dtype=jnp.int32))
    return result.reshape(NB * B, NC)
```

```python
import jax
import jax.numpy as jnp
from jax import lax
from jax.experimental import pallas as pl
from jax.experimental.pallas import tpu as pltpu
from jax.sharding import PartitionSpec as P

MESH = pl.DeviceIdType.MESH
BF = jnp.bfloat16
F32 = jnp.float32
T = 64
RB = 32
MT = 256
ROWS = RB * T
HALF = 512
WIDE = 2 * HALF
GROUPS = 2


def kernel(
    table, meta, p_hbm, l_hbm, s_hbm, out,
    praw, aloc, asec, pc, pp, mp, r1a, r1b, r1m, s1, s1m, r2, r2m, s2, s2m, rx, rxm, qc, qm, mf,
    d0, d1, dense, ab0, ab1, acc,
    load_sem, send_sem, recv_sem, osend, orecv, olocal,
):
    r = lax.axis_index("rows")
    c = lax.axis_index("cols")
    y, xl, z = r // 8, (r // 4) % 2, r % 4
    xh, core = c // 2, c % 2
    x = xh * 2 + xl

    def y_peer(j):
        return (((y + j) % 4 * 2 + xl) * 4 + z, c)

    def z_peer(j):
        return ((y * 2 + xl) * 4 + (z + j) % 4, c)

    def x_peer(j):
        q = (x + j) % 4
        return ((y * 2 + q % 2) * 4 + z, (q // 2) * 2 + core)

    core_peer = (r, xh * 2 + 1 - core)

    loads = [
        pltpu.make_async_copy(p_hbm, praw, load_sem.at[0]),
        pltpu.make_async_copy(l_hbm, aloc.at[pl.ds(0, 768)], load_sem.at[1]),
        pltpu.make_async_copy(s_hbm, asec.at[pl.ds(0, 768)], load_sem.at[2]),
    ]
    for load in loads:
        load.start()

    barrier = pltpu.get_barrier_semaphore()
    for peer in [f(j) for f in (y_peer, z_peer, x_peer) for j in (1, 2, 3)] + [core_peer]:
        pl.semaphore_signal(barrier, inc=1, device_id=peer, device_id_type=MESH)

    aloc[768] = jnp.zeros((T, T), BF)
    asec[768] = jnp.zeros((T, T), BF)

    loads[0].wait()

    def compact(k, _):
        rows = pl.ds(pl.multiple_of(k * T, T), T)
        pc[rows, :] = jnp.concatenate([praw[2 * k], praw[2 * k + 1]], axis=1)
        return 0

    lax.fori_loop(0, RB, compact, 0)

    def owner(s):
        o = table[3072 + s]
        return o // 8, (o // 4) % 2, o % 4

    sent = []

    def remote(src, dst, peer):
        i = len(sent)
        copy = pltpu.make_async_remote_copy(
            src_ref=src, dst_ref=dst, send_sem=send_sem.at[i], recv_sem=recv_sem.at[i],
            device_id=peer, device_id_type=MESH,
        )
        copy.start()
        sent.append(copy)
        return copy

    def rows_at(base, index, size):
        return pl.ds(pl.multiple_of(base + index * size, size), size)

    pl.semaphore_wait(barrier, 10)

    stage1 = []
    for j in (1, 2, 3):
        stage1.append(remote(pc.at[rows_at(0, (y + j) % 4, 256)], r1a.at[j], y_peer(j)))
        stage1.append(remote(pc.at[rows_at(1024, (z + j) % 4, 256)], r1b.at[j], z_peer(j)))
        stage1.append(remote(meta, r1m.at[j], y_peer(j)))
    partner = [remote(pc, pp, x_peer(2)), remote(meta, mp, x_peer(2))]
    r1a[0] = pc[rows_at(0, y, 256)]
    r1b[0] = pc[rows_at(1024, z, 256)]
    r1m[0] = meta[...]

    stage2, stage3, stage4, stage5 = [], [], [[], []], [[], []]

    def step1():
        for copy in stage1:
            copy.wait_recv()
        for s in range(GROUPS):
            oy, ox, oz = owner(s)
            s1[s, 0] = r1a[(y + 4 - oy) % 4]
            s1[s, 1] = r1b[(z + 4 - oz) % 4]
            s1m[s] = r1m[(y + 4 - oy) % 4]
        for s in range(GROUPS):
            for j in (1, 2, 3):
                stage2.append(remote(s1.at[s, 0, rows_at(0, (z + j) % 4, T)], r2.at[s, 0, j], z_peer(j)))
                stage2.append(remote(s1.at[s, 1, rows_at(0, (y + j) % 4, T)], r2.at[s, 1, j], y_peer(j)))
        for j in (1, 2, 3):
            stage2.append(remote(s1m, r2m.at[j], z_peer(j)))
        for s in range(GROUPS):
            r2[s, 0, 0] = s1[s, 0, rows_at(0, z, T)]
            r2[s, 1, 0] = s1[s, 1, rows_at(0, y, T)]
        r2m[0] = s1m[...]

    def step2():
        for copy in stage2:
            copy.wait_recv()
        for s in range(GROUPS):
            oy, ox, oz = owner(s)
            s2[s, 0] = r2[s, 0, (z + 4 - oz) % 4]
            s2[s, 1] = r2[s, 1, (y + 4 - oy) % 4]
            s2m[s] = r2m[(z + 4 - oz) % 4, s]
        for s in range(GROUPS):
            for j in (1, 2, 3):
                stage3.append(remote(s2.at[s], rx.at[s, j], x_peer(j)))
        for j in (1, 2, 3):
            stage3.append(remote(s2m, rxm.at[j], x_peer(j)))
        for s in range(GROUPS):
            rx[s, 0] = s2[s]
        rxm[0] = s2m[...]

    def step3():
        for copy in stage3:
            copy.wait_recv()
        for s in range(GROUPS):
            oy, ox, oz = owner(s)
            for h in range(2):
                slot = (x + 4 - (h * 2 + ox)) % 4
                qc[s, h, rows_at(0, y * 4 + z, T)] = rx[s, slot, 0]
                qc[s, h, rows_at(1024, z * 4 + y, T)] = rx[s, slot, 1]
                qm[s, h] = rxm[slot, s]
        for s in range(GROUPS):
            for j in (1, 2, 3):
                first = qc.at[s, :, rows_at(0, y * 4 + z, T)]
                second = qc.at[s, :, rows_at(1024, z * 4 + y, T)]
                stage4[s].append(remote(first, first, z_peer(j)))
                stage4[s].append(remote(second, second, y_peer(j)))

    def step4(s):
        for copy in stage4[s]:
            copy.wait_recv()
        for j in (1, 2, 3):
            first = qc.at[s, :, rows_at(0, y, 256)]
            second = qc.at[s, :, rows_at(1024, z, 256)]
            stage5[s].append(remote(first, first, y_peer(j)))
            stage5[s].append(remote(second, second, z_peer(j)))

    def step5(s):
        for copy in stage5[s]:
            copy.wait_recv()

    def spread(src, cols, dst, h):
        mf[...] = cols.astype(F32)
        lane = lax.broadcasted_iota(jnp.int32, (16, 128), 1)
        side = (lane >= T).astype(F32)

        def body(k, _):
            row = jnp.broadcast_to(mf[pl.ds(k, 1), :], (16, 128))
            swapped = jnp.concatenate([row[:, T:], row[:, :T]], axis=1)
            masks = [
                (jnp.where(row == side + 2.0 * p, 1.0, 0.0).astype(BF),
                 jnp.where(swapped == side + 2.0 * p, 1.0, 0.0).astype(BF))
                for p in range(4)
            ]
            for q in range(4):
                rows = pl.ds(pl.multiple_of(k * T + q * 16, 16), 16)
                t = src(rows)
                u = jnp.concatenate([t[:, T:], t[:, :T]], axis=1)
                for p in range(4):
                    dst[rows, h * HALF + p * 128 : h * HALF + (p + 1) * 128] = t * masks[p][0] + u * masks[p][1]
            return 0

        lax.fori_loop(0, RB, body, 0)

    def fill(src, which, m, stores):
        for b in range(4):
            base = which * 1024 + (m * 4 + b) * RB
            for p in range(16):
                pair = jnp.concatenate([src[table[base + 2 * p]], src[table[base + 2 * p + 1]]], axis=1)
                for ref, start in stores:
                    ref[pl.ds(start + b * T, T), p * 128 : (p + 1) * 128] = pair

    def rows_of(m):
        return pl.ds(pl.multiple_of(m * MT, MT), MT)

    spread(lambda rows: pc[rows, :], meta[...], d0, 0)
    loads[1].wait()

    def pass1(m, ab):
        for n in range(2):
            cols = slice(n * 256, (n + 1) * 256)
            acc[rows_of(m), cols] = jnp.dot(ab[...], d0[:, cols], preferred_element_type=F32)

    def start_of(m):
        return pl.multiple_of(m * MT, MT)

    fill(aloc, 0, 0, [(ab0, 0), (dense, 0)])

    def loop1(jj, _):
        m = 2 * jj
        fill(aloc, 0, m + 1, [(ab1, 0), (dense, start_of(m + 1))])
        pass1(m, ab0)
        after = jnp.minimum(m + 2, 7)
        fill(aloc, 0, after, [(ab0, 0), (dense, start_of(after))])
        pass1(m + 1, ab1)
        return 0

    lax.fori_loop(0, 1, loop1, 0)
    step1()
    lax.fori_loop(1, 2, loop1, 0)
    step2()
    lax.fori_loop(2, 3, loop1, 0)
    step3()
    lax.fori_loop(3, 4, loop1, 0)
    step4(0)
    step4(1)

    for copy in partner:
        copy.wait_recv()
    spread(lambda rows: pp[rows, :], mp[...], d0, 1)

    def loop2(m, _):
        for n in range(2, 4):
            cols = slice(n * 256, (n + 1) * 256)
            acc[rows_of(m), cols] = jnp.dot(dense[rows_of(m), :], d0[:, cols], preferred_element_type=F32)
        return 0

    lax.fori_loop(0, 8, loop2, 0)

    loads[2].wait()
    fill(asec, 1, 0, [(ab0, 0)])
    step5(0)
    for h in range(2):
        side = xh * (1 - h) + (1 - xh) * h
        spread(lambda rows: qc[0, side, rows, :], qm[0, side], d1, h)

    def pass3(m, ab):
        for n in range(4):
            cols = slice(n * 256, (n + 1) * 256)
            acc[rows_of(m), cols] += jnp.dot(ab[...], d1[:, cols], preferred_element_type=F32)

    def loop3(jj, _):
        m = 2 * jj
        fill(asec, 1, m + 1, [(ab1, 0)])
        pass3(m, ab0)
        fill(asec, 1, jnp.minimum(m + 2, 7), [(ab0, 0)])
        pass3(m + 1, ab1)
        return 0

    lax.fori_loop(0, 4, loop3, 0)

    fill(asec, 2, 0, [(ab0, 0)])
    step5(1)
    for h in range(2):
        side = xh * (1 - h) + (1 - xh) * h
        spread(lambda rows: qc[1, side, rows, :], qm[1, side], d0, h)

    def results(m):
        copies = []
        for h in range(2):
            side = xh * (1 - h) + (1 - xh) * h
            src = dense.at[rows_of(m), pl.ds(h * HALF, HALF)]
            dst = out.at[rows_of(m), pl.ds(pl.multiple_of((side * 2 + core) * HALF, HALF), HALF)]
            copies.append((
                pltpu.make_async_copy(src, dst, olocal.at[m, h]),
                pltpu.make_async_remote_copy(
                    src_ref=src, dst_ref=dst, send_sem=osend.at[m, h], recv_sem=orecv.at[m, h],
                    device_id=core_peer, device_id_type=MESH,
                ),
            ))
        return copies

    def pass4(m, ab):
        for n in range(4):
            cols = slice(n * 256, (n + 1) * 256)
            total = acc[rows_of(m), cols] + jnp.dot(ab[...], d0[:, cols], preferred_element_type=F32)
            dense[rows_of(m), cols] = total.astype(BF)
        for local, away in results(m):
            away.start()
            local.start()

    def loop4(jj, _):
        m = 2 * jj
        fill(asec, 2, m + 1, [(ab1, 0)])
        pass4(m, ab0)
        fill(asec, 2, jnp.minimum(m + 2, 7), [(ab0, 0)])
        pass4(m + 1, ab1)
        return 0

    lax.fori_loop(0, 4, loop4, 0)

    def finish(m, _):
        for local, away in results(m):
            local.wait()
            away.wait()
        return 0

    lax.fori_loop(0, 8, finish, 0)
    for copy in sent:
        copy.wait_send()


def per_device(local_tiles, local_cols, section_tiles, section_cols, owners, prol_tiles, prol_cols):
    slots = jnp.arange(RB, dtype=jnp.int32)
    k = local_cols.shape[1]
    place = (slots[:, None] * k + jnp.arange(k, dtype=jnp.int32)[None, :])[:, :, None]
    local = jnp.min(jnp.where(local_cols[:, :, None] == slots, place, RB * k), axis=1)
    ks = section_cols.shape[2]
    place = jnp.arange(RB * GROUPS * ks, dtype=jnp.int32).reshape(RB, GROUPS, ks)[:, :, :, None]
    section = jnp.min(jnp.where(section_cols[:, :, :, None] == slots, place, RB * k), axis=2)
    table = jnp.concatenate([local.reshape(-1), section.transpose(1, 0, 2).reshape(-1), owners])
    meta = jnp.where(jnp.arange(128)[None, :] < T, prol_cols[:, 0:1], prol_cols[:, 1:2]).astype(BF)

    vmem = pl.BlockSpec(memory_space=pltpu.VMEM)
    smem = pl.BlockSpec(memory_space=pltpu.SMEM)
    hbm = pl.BlockSpec(memory_space=pl.ANY)
    v = pltpu.VMEM
    copies = 64
    return pl.pallas_call(
        kernel,
        out_shape=jax.ShapeDtypeStruct((ROWS, 2048), BF),
        in_specs=[smem, vmem, hbm, hbm, hbm],
        out_specs=hbm,
        scratch_shapes=[
            v((64, T, T), BF), v((769, T, T), BF), v((769, T, T), BF),
            v((ROWS, 128), BF), v((ROWS, 128), BF), v((RB, 128), BF),
            v((4, 256, 128), BF), v((4, 256, 128), BF), v((4, RB, 128), BF),
            v((2, 2, 256, 128), BF), v((2, RB, 128), BF),
            v((2, 2, 4, T, 128), BF), v((4, 2, RB, 128), BF),
            v((2, 2, T, 128), BF), v((2, RB, 128), BF),
            v((2, 4, 2, T, 128), BF), v((4, 2, RB, 128), BF),
            v((2, 2, ROWS, 128), BF), v((2, 2, RB, 128), BF), v((RB, 128), F32),
            v((ROWS, WIDE), BF), v((ROWS, WIDE), BF), v((ROWS, ROWS), BF),
            v((MT, ROWS), BF), v((MT, ROWS), BF), v((ROWS, WIDE), F32),
            pltpu.SemaphoreType.DMA((3,)),
            pltpu.SemaphoreType.DMA((copies,)), pltpu.SemaphoreType.DMA((copies,)),
            pltpu.SemaphoreType.DMA((8, 2)), pltpu.SemaphoreType.DMA((8, 2)), pltpu.SemaphoreType.DMA((8, 2)),
        ],
        compiler_params=pltpu.CompilerParams(
            collective_id=0, has_side_effects=True, vmem_limit_bytes=60 * 2**20
        ),
        name="galerkin",
    )(table, meta, prol_tiles.reshape(64, T, T), local_tiles.reshape(768, T, T), section_tiles.reshape(768, T, T))


def solution(mesh):
    in_specs = (
        P("rows", None, None, None),
        P("rows", None),
        P("rows", None, None, None, None),
        P("rows", None, None),
        P(),
        P("rows", "cols", None, None),
        P("rows", "cols"),
    )
    return jax.shard_map(
        per_device, mesh=mesh, in_specs=in_specs, out_specs=P("rows", None), check_vma=False
    )
```

```python
import jax
import jax.numpy as jnp
from jax import lax
from jax.experimental import pallas as pl
from jax.experimental.pallas import tpu as pltpu
from jax.sharding import PartitionSpec as P

MESH = pl.DeviceIdType.MESH
BF = jnp.bfloat16
F32 = jnp.float32
T = 64
RB = 32
MT = 256
ROWS = RB * T
HALF = 512
WIDE = 2 * HALF
GROUPS = 2
K = 24
KS = 12


def kernel(
    lcols, scols, pcols, owners, p_hbm, l_hbm, s_hbm, out,
    praw, aloc, asec, pc, pp, meta, mp, r1a, r1b, r1m, s1, s1m, r2_0, r2_1, r2m_0, r2m_1, s2, s2m,
    rx_0, rx_1, rxm_0, rxm_1, qc, qm, mf,
    d0, d1, ab0, ab1, acc, vtable, table,
    load_sem, send_sem, recv_sem, osend, orecv,
):
    r = lax.axis_index("rows")
    c = lax.axis_index("cols")
    y, xl, z = r // 8, (r // 4) % 2, r % 4
    xh, core = c // 2, c % 2
    x = xh * 2 + xl

    def y_peer(j):
        return (((y + j) % 4 * 2 + xl) * 4 + z, c)

    def z_peer(j):
        return ((y * 2 + xl) * 4 + (z + j) % 4, c)

    def x_peer(j):
        q = (x + j) % 4
        return ((y * 2 + q % 2) * 4 + z, (q // 2) * 2 + core)

    core_peer = (r, xh * 2 + 1 - core)
    r2, r2m, rx, rxm = (r2_0, r2_1), (r2m_0, r2m_1), (rx_0, rx_1), (rxm_0, rxm_1)

    load_p = pltpu.make_async_copy(p_hbm, praw, load_sem.at[0])
    load_l = pltpu.make_async_copy(l_hbm, aloc.at[:, pl.ds(0, K)], load_sem.at[1])
    load_s = [
        pltpu.make_async_copy(s_hbm.at[:, 0], asec.at[:, pl.ds(0, KS)], load_sem.at[2]),
        pltpu.make_async_copy(s_hbm.at[:, 1], aloc.at[:, pl.ds(0, KS)], load_sem.at[3]),
    ]
    load_p.start()
    load_l.start()
    load_s[0].start()

    barrier = pltpu.get_barrier_semaphore()
    for peer in [f(j) for f in (y_peer, z_peer, x_peer) for j in (1, 2, 3)] + [core_peer]:
        pl.semaphore_signal(barrier, inc=1, device_id=peer, device_id_type=MESH)

    sub = lax.broadcasted_iota(jnp.int32, (RB, RB), 0)
    lane = lax.broadcasted_iota(jnp.int32, (RB, RB), 1)
    first, second = [
        jnp.sum(jnp.where(sub == lane, pcols[j : j + 1, :], 0).astype(F32), axis=1, keepdims=True) for j in range(2)
    ]
    meta[...] = jnp.where(lax.broadcasted_iota(jnp.int32, (RB, 128), 1) < T, first, second).astype(BF)

    def owner(s):
        o = owners[s]
        return o // 8, (o // 4) % 2, o % 4

    sent = []

    def remote(src, dst, peer):
        i = len(sent)
        copy = pltpu.make_async_remote_copy(
            src_ref=src, dst_ref=dst, send_sem=send_sem.at[i], recv_sem=recv_sem.at[i],
            device_id=peer, device_id_type=MESH,
        )
        copy.start()
        sent.append(copy)
        return copy

    def rows_at(base, index, size):
        return pl.ds(pl.multiple_of(base + index * size, size), size)

    load_p.wait()

    def compact(k, _):
        rows = pl.ds(pl.multiple_of(k * T, T), T)
        pc[rows, :] = jnp.concatenate([praw[k, 0], praw[k, 1]], axis=1)
        return 0

    lax.fori_loop(0, RB, compact, 0, unroll=4)
    pl.semaphore_wait(barrier, 10)

    stage1 = []
    for j in (1, 2, 3):
        stage1.append(remote(pc.at[rows_at(0, (y + j) % 4, 256)], r1a.at[j], y_peer(j)))
        stage1.append(remote(pc.at[rows_at(1024, (z + j) % 4, 256)], r1b.at[j], z_peer(j)))
        stage1.append(remote(meta, r1m.at[j], y_peer(j)))
    half = pl.ds(0, 1024)
    partner = [remote(pc.at[half], pp.at[half], x_peer(2)), remote(meta, mp, x_peer(2))]
    r1a[0] = pc[rows_at(0, y, 256)]
    r1b[0] = pc[rows_at(1024, z, 256)]
    r1m[0] = meta[...]

    stage2, stage3, stage4, stage5 = [[], []], [[], []], [[], []], [[], []]

    def step1():
        for copy in stage1:
            copy.wait_recv()
        for s in range(GROUPS):
            oy, ox, oz = owner(s)
            s1[s, 0] = r1a[(y + 4 - oy) % 4]
            s1[s, 1] = r1b[(z + 4 - oz) % 4]
            s1m[s] = r1m[(y + 4 - oy) % 4]
            for j in (1, 2, 3):
                stage2[s].append(remote(s1.at[s, 0, rows_at(0, (z + j) % 4, T)], r2[s].at[0, j], z_peer(j)))
                stage2[s].append(remote(s1.at[s, 1, rows_at(0, (y + j) % 4, T)], r2[s].at[1, j], y_peer(j)))
                stage2[s].append(remote(s1m.at[s], r2m[s].at[j], z_peer(j)))
            r2[s][0, 0] = s1[s, 0, rows_at(0, z, T)]
            r2[s][1, 0] = s1[s, 1, rows_at(0, y, T)]
            r2m[s][0] = s1m[s]

    def step2(s):
        for copy in stage2[s]:
            copy.wait_recv()
        oy, ox, oz = owner(s)
        s2[s, 0] = r2[s][0, (z + 4 - oz) % 4]
        s2[s, 1] = r2[s][1, (y + 4 - oy) % 4]
        s2m[s] = r2m[s][(z + 4 - oz) % 4]
        for j in (1, 2, 3):
            stage3[s].append(remote(s2.at[s], rx[s].at[j], x_peer(j)))
            stage3[s].append(remote(s2m.at[s], rxm[s].at[j], x_peer(j)))
        rx[s][0] = s2[s]
        rxm[s][0] = s2m[s]

    def step3(s):
        for copy in stage3[s]:
            copy.wait_recv()
        oy, ox, oz = owner(s)
        for h in range(2):
            slot = (x + 4 - (h * 2 + ox)) % 4
            qc[s, h, rows_at(0, y * 4 + z, T)] = rx[s][slot, 0]
            qc[s, h, rows_at(1024, z * 4 + y, T)] = rx[s][slot, 1]
            qm[s, h] = rxm[s][slot]
        first = qc.at[s, :, rows_at(0, y * 4 + z, T)]
        second = qc.at[s, :, rows_at(1024, z * 4 + y, T)]
        for j in (1, 2, 3):
            stage4[s].append(remote(first, first, z_peer(j)))
            stage4[s].append(remote(second, second, y_peer(j)))

    def step4(s):
        for copy in stage4[s]:
            copy.wait_recv()
        first = qc.at[s, :, rows_at(0, y, 256)]
        second = qc.at[s, :, rows_at(1024, z, 256)]
        for j in (1, 2, 3):
            stage5[s].append(remote(first, first, y_peer(j)))
            stage5[s].append(remote(second, second, z_peer(j)))

    def step5(s):
        for copy in stage5[s]:
            copy.wait_recv()

    tile = jnp.full((RB, RB), K, jnp.int32)
    for k in range(K):
        tile = jnp.where(lcols[k : k + 1, :] == sub, k, tile)
    vtable[0:RB, 0:RB] = tile
    for s in range(GROUPS):
        tile = jnp.full((RB, RB), K if s else KS, jnp.int32)
        for k in range(KS):
            tile = jnp.where(scols[k][s : s + 1, :] == sub, k, tile)
        vtable[RB * (s + 1) : RB * (s + 2), 0:RB] = tile
    to_scalar = pltpu.make_async_copy(vtable, table, load_sem.at[4])
    to_scalar.start()

    def clear(i, _):
        aloc[i, K] = jnp.zeros((T, T), BF)
        asec[i, KS] = jnp.zeros((T, T), BF)
        return 0

    lax.fori_loop(0, RB, clear, 0, unroll=4)

    side = (lax.broadcasted_iota(jnp.int32, (16, 128), 1) >= T).astype(F32)
    slots = [(side + 2.0 * p).astype(BF) for p in range(4)]

    def spread(src, cols, dst, h):
        mf[...] = cols.astype(F32)

        def body(k, _):
            row = jnp.broadcast_to(mf[pl.ds(k, 1), :], (16, 128))
            swapped = jnp.concatenate([row[:, T:], row[:, :T]], axis=1).astype(BF)
            row = row.astype(BF)
            masks = [(row == slots[p], swapped == slots[p]) for p in range(4)]
            for q in range(4):
                rows = pl.ds(pl.multiple_of(k * T + q * 16, 16), 16)
                t = src(rows)
                u = jnp.concatenate([t[:, T:], t[:, :T]], axis=1)
                for p in range(4):
                    dst[rows, h * HALF + p * 128 : h * HALF + (p + 1) * 128] = jnp.where(
                        masks[p][0], t, jnp.where(masks[p][1], u, jnp.zeros_like(t))
                    )
            return 0

        lax.fori_loop(0, RB, body, 0, unroll=8)

    def fill(src, which, m, dst):
        for b in range(4):
            i = m * 4 + b
            for p in range(16):
                dst[b * T : (b + 1) * T, p * 128 : (p + 1) * 128] = jnp.concatenate(
                    [src[i, table[which * RB + 2 * p, i]], src[i, table[which * RB + 2 * p + 1, i]]], axis=1
                )

    def rows_of(m):
        return pl.ds(pl.multiple_of(m * MT, MT), MT)

    def multiply(src, which, use, points=()):
        fill(src, which, 0, ab0)

        def pair(jj, _):
            m = 2 * jj
            fill(src, which, m + 1, ab1)
            use(m, ab0)
            fill(src, which, jnp.minimum(m + 2, 7), ab0)
            use(m + 1, ab1)
            return 0

        start = 0
        for stop, point in points:
            lax.fori_loop(start, stop, pair, 0)
            point()
            start = stop
        lax.fori_loop(start, 4, pair, 0)

    spread(lambda rows: pc[rows, :], meta[...], d0, 0)
    to_scalar.wait()
    load_l.wait()

    def pass1(m, ab):
        for n in range(2):
            cols = slice(n * 256, (n + 1) * 256)
            acc[rows_of(m), cols] = jnp.dot(ab[...], d0[:, cols], preferred_element_type=F32)

    other = pl.ds(1024, 1024)

    def point2():
        step2(0)
        partner.append(remote(pc.at[other], pp.at[other], x_peer(2)))

    def point3():
        step2(1)
        step3(0)

    multiply(aloc, 0, pass1, [(1, step1), (2, point2), (3, point3)])
    step4(0)
    step3(1)

    for copy in partner:
        copy.wait_recv()
    spread(lambda rows: pp[rows, :], mp[...], d0, 1)

    def pass2(m, ab):
        for n in range(2, 4):
            cols = slice(n * 256, (n + 1) * 256)
            acc[rows_of(m), cols] = jnp.dot(ab[...], d0[:, cols], preferred_element_type=F32)

    multiply(aloc, 0, pass2)

    load_s[1].start()
    load_s[0].wait()
    sides = [xh, 1 - xh]
    step5(0)
    step4(1)
    for h in range(2):
        spread(lambda rows: qc[0, sides[h], rows, :], qm[0, sides[h]], d1, h)

    def pass3(m, ab):
        for n in range(4):
            cols = slice(n * 256, (n + 1) * 256)
            acc[rows_of(m), cols] += jnp.dot(ab[...], d1[:, cols], preferred_element_type=F32)

    multiply(asec, 1, pass3)

    load_s[1].wait()
    step5(1)
    for h in range(2):
        spread(lambda rows: qc[1, sides[h], rows, :], qm[1, sides[h]], d0, h)

    def place(m, h):
        return rows_of(m), pl.ds(pl.multiple_of((sides[h] * 2 + core) * HALF, HALF), HALF)

    def result(m, h):
        ref = out.at[place(m, h)]
        return pltpu.make_async_remote_copy(
            src_ref=ref, dst_ref=ref, send_sem=osend.at[m, h], recv_sem=orecv.at[m, h],
            device_id=core_peer, device_id_type=MESH,
        )

    def pass4(m, ab):
        for h in range(2):
            cols = slice(h * HALF, (h + 1) * HALF)
            total = acc[rows_of(m), cols] + jnp.dot(ab[...], d0[:, cols], preferred_element_type=F32)
            out[place(m, h)] = total.astype(BF)
            result(m, h).start()

    multiply(aloc, 2, pass4)

    def finish(m, _):
        for h in range(2):
            result(m, h).wait()
        return 0

    lax.fori_loop(0, 8, finish, 0)
    for copy in sent:
        copy.wait_send()


def per_device(local_tiles, local_cols, section_tiles, section_cols, owners, prol_tiles, prol_cols):
    vmem = pl.BlockSpec(memory_space=pltpu.VMEM)
    smem = pl.BlockSpec(memory_space=pltpu.SMEM)
    hbm = pl.BlockSpec(memory_space=pl.ANY)
    v = pltpu.VMEM
    copies = 72
    return pl.pallas_call(
        kernel,
        out_shape=pltpu.VMEM((ROWS, 2048), BF),
        in_specs=[vmem, vmem, vmem, smem, hbm, hbm, hbm],
        out_specs=pl.BlockSpec(memory_space=pltpu.VMEM),
        scratch_shapes=[
            v((RB, 2, T, T), BF), v((RB, K + 1, T, T), BF), v((RB, KS + 1, T, T), BF),
            v((ROWS, 128), BF), v((ROWS, 128), BF), v((RB, 128), BF), v((RB, 128), BF),
            v((4, 256, 128), BF), v((4, 256, 128), BF), v((4, RB, 128), BF),
            v((2, 2, 256, 128), BF), v((2, RB, 128), BF),
            v((2, 4, T, 128), BF), v((2, 4, T, 128), BF), v((4, RB, 128), BF), v((4, RB, 128), BF),
            v((2, 2, T, 128), BF), v((2, RB, 128), BF),
            v((4, 2, T, 128), BF), v((4, 2, T, 128), BF), v((4, RB, 128), BF), v((4, RB, 128), BF),
            v((2, 2, ROWS, 128), BF), v((2, 2, RB, 128), BF), v((RB, 128), F32),
            v((ROWS, WIDE), BF), v((ROWS, WIDE), BF),
            v((MT, ROWS), BF), v((MT, ROWS), BF), v((ROWS, WIDE), F32),
            v((3 * RB, 128), jnp.int32), pltpu.SMEM((3 * RB, 128), jnp.int32),
            pltpu.SemaphoreType.DMA((5,)),
            pltpu.SemaphoreType.DMA((copies,)), pltpu.SemaphoreType.DMA((copies,)),
            pltpu.SemaphoreType.DMA((8, 2)), pltpu.SemaphoreType.DMA((8, 2)),
        ],
        compiler_params=pltpu.CompilerParams(
            collective_id=0, has_side_effects=True, vmem_limit_bytes=46 * 2**20
        ),
        name="galerkin",
    )(local_cols.T, section_cols.transpose(2, 1, 0), prol_cols.T, owners, prol_tiles, local_tiles, section_tiles)


def solution(mesh):
    in_specs = (
        P("rows", None, None, None),
        P("rows", None),
        P("rows", None, None, None, None),
        P("rows", None, None),
        P(),
        P("rows", "cols", None, None),
        P("rows", "cols"),
    )
    return jax.shard_map(
        per_device, mesh=mesh, in_specs=in_specs, out_specs=P("rows", None), check_vma=False
    )
```

```python
import jax
import jax.numpy as jnp
from jax import lax
from jax.experimental import pallas as pl
from jax.experimental.pallas import tpu as pltpu
from jax.sharding import PartitionSpec as P

MESH = pl.DeviceIdType.MESH
BF = jnp.bfloat16
F32 = jnp.float32
T = 64
RB = 32
K = 24
KS = 12
MT = 256
ROWS = RB * T
DEPTH = ROWS // 2
HALF = 512
WIDE = 2 * HALF
UNITS = [(0, 0), (0, 1), (1, 0), (1, 1)]
COPIES = 128


def kernel(lcols, scols, pcols, owners, p_hbm, l_hbm, s_hbm, out, *scratch):
    refs = iter(scratch)

    def take(n):
        return [next(refs) for _ in range(n)]

    praw, aloc, asec, pc, pp, meta, mp, mown, mpart, mq = take(10)
    r1a, r1b = take(2), take(2)
    r1m, s1, s1m = take(3)
    r2, r2m = take(4), take(2)
    s2, s2m = take(2)
    rx, rxm = take(4), take(2)
    qc, d0, d1, ab0, ab1, acc, vtable, table = take(8)
    load_sem, send_sem, recv_sem, osend, orecv = take(5)

    r = lax.axis_index("rows")
    c = lax.axis_index("cols")
    y, xl, z = r // 8, (r // 4) % 2, r % 4
    xh, core = c // 2, c % 2
    x = xh * 2 + xl
    sides = [xh, 1 - xh]

    def y_peer(j):
        return (((y + j) % 4 * 2 + xl) * 4 + z, c)

    def z_peer(j):
        return ((y * 2 + xl) * 4 + (z + j) % 4, c)

    def x_peer(j):
        q = (x + j) % 4
        return ((y * 2 + q % 2) * 4 + z, (q // 2) * 2 + core)

    core_peer = (r, xh * 2 + 1 - core)

    load_p = pltpu.make_async_copy(p_hbm, praw, load_sem.at[0])
    load_l = pltpu.make_async_copy(l_hbm, aloc.at[:, pl.ds(0, K)], load_sem.at[1])
    load_s = [
        pltpu.make_async_copy(s_hbm.at[:, 0], asec.at[:, pl.ds(0, KS)], load_sem.at[2]),
        pltpu.make_async_copy(s_hbm.at[:, 1], aloc.at[:, pl.ds(0, KS)], load_sem.at[3]),
    ]
    load_p.start()
    load_l.start()
    load_s[0].start()

    barrier = pltpu.get_barrier_semaphore()
    for peer in [f(j) for f in (y_peer, z_peer, x_peer) for j in (1, 2, 3)] + [core_peer]:
        pl.semaphore_signal(barrier, inc=1, device_id=peer, device_id_type=MESH)

    sub = lax.broadcasted_iota(jnp.int32, (RB, RB), 0)
    lane = lax.broadcasted_iota(jnp.int32, (RB, RB), 1)
    first, second = [
        jnp.sum(jnp.where(sub == lane, pcols[j : j + 1, :], 0).astype(F32), axis=1, keepdims=True) for j in range(2)
    ]
    mown[...] = jnp.where(lax.broadcasted_iota(jnp.int32, (RB, 128), 1) < T, first, second)
    meta[...] = mown[...].astype(BF)

    def owner(s):
        o = owners[s]
        return o // 8, (o // 4) % 2, o % 4

    sent = []

    def remote(src, dst, peer):
        i = len(sent)
        copy = pltpu.make_async_remote_copy(
            src_ref=src, dst_ref=dst, send_sem=send_sem.at[i], recv_sem=recv_sem.at[i],
            device_id=peer, device_id_type=MESH,
        )
        copy.start()
        sent.append(copy)
        return copy

    def rows_at(base, index, size):
        return pl.ds(pl.multiple_of(base + index * size, size), size)

    load_p.wait()

    def compact(k, _):
        rows = pl.ds(pl.multiple_of(k * T, T), T)
        pc[rows, :] = jnp.concatenate([praw[k, 0], praw[k, 1]], axis=1)
        return 0

    lax.fori_loop(0, RB, compact, 0, unroll=4)
    pl.semaphore_wait(barrier, 10)

    base_a = [u * DEPTH for u in range(2)]
    base_b = [u * DEPTH + DEPTH // 2 for u in range(2)]
    stage1 = [[], []]
    for h in range(2):
        for j in (1, 2, 3):
            stage1[h].append(remote(pc.at[rows_at(base_a[h], (y + j) % 4, 128)], r1a[h].at[j], y_peer(j)))
            stage1[h].append(remote(pc.at[rows_at(base_b[h], (z + j) % 4, 128)], r1b[h].at[j], z_peer(j)))
            if h == 0:
                stage1[h].append(remote(meta, r1m.at[j], y_peer(j)))
    halves = [pl.ds(0, DEPTH), pl.ds(DEPTH, DEPTH)]
    partner = [[remote(meta, mp, x_peer(2)), remote(pc.at[halves[0]], pp.at[halves[0]], x_peer(2))]]
    for h in range(2):
        r1a[h][0] = pc[rows_at(base_a[h], y, 128)]
        r1b[h][0] = pc[rows_at(base_b[h], z, 128)]
    r1m[0] = meta[...]

    stage2, stage3, stage4, stage5 = [[[] for _ in UNITS] for _ in range(4)]

    def step1(h):
        for copy in stage1[h]:
            copy.wait_recv()
        for s in range(2):
            u = 2 * s + h
            oy, ox, oz = owner(s)
            s1[u, 0] = r1a[h][(y + 4 - oy) % 4]
            s1[u, 1] = r1b[h][(z + 4 - oz) % 4]
            if h == 0:
                s1m[s] = r1m[(y + 4 - oy) % 4]
            for j in (1, 2, 3):
                stage2[u].append(remote(s1.at[u, 0, rows_at(0, (z + j) % 4, 32)], r2[u].at[0, j], z_peer(j)))
                stage2[u].append(remote(s1.at[u, 1, rows_at(0, (y + j) % 4, 32)], r2[u].at[1, j], y_peer(j)))
                if h == 0:
                    stage2[u].append(remote(s1m.at[s], r2m[s].at[j], z_peer(j)))
            r2[u][0, 0] = s1[u, 0, rows_at(0, z, 32)]
            r2[u][1, 0] = s1[u, 1, rows_at(0, y, 32)]
            if h == 0:
                r2m[s][0] = s1m[s]

    def step2(u):
        s, h = UNITS[u]
        for copy in stage2[u]:
            copy.wait_recv()
        oy, ox, oz = owner(s)
        s2[u, 0] = r2[u][0, (z + 4 - oz) % 4]
        s2[u, 1] = r2[u][1, (y + 4 - oy) % 4]
        for j in (1, 2, 3):
            stage3[u].append(remote(s2.at[u], rx[u].at[j], x_peer(j)))
        rx[u][0] = s2[u]
        if h == 0:
            s2m[s] = r2m[s][(z + 4 - oz) % 4]
            for j in (1, 2, 3):
                stage3[u].append(remote(s2m.at[s], rxm[s].at[j], x_peer(j)))
            rxm[s][0] = s2m[s]

    def step3(u):
        s, h = UNITS[u]
        for copy in stage3[u]:
            copy.wait_recv()
        oy, ox, oz = owner(s)
        mine_a = rows_at(base_a[h], y * 4 + z, 32)
        mine_b = rows_at(base_b[h], z * 4 + y, 32)
        for side in range(2):
            slot = (x + 4 - (side * 2 + ox)) % 4
            qc[s, side, mine_a] = rx[u][slot, 0]
            qc[s, side, mine_b] = rx[u][slot, 1]
            if h == 0:
                mq[s, side] = rxm[s][slot].astype(F32)
        piece_a, piece_b = qc.at[s, :, mine_a], qc.at[s, :, mine_b]
        for j in (1, 2, 3):
            stage4[u].append(remote(piece_a, piece_a, z_peer(j)))
            stage4[u].append(remote(piece_b, piece_b, y_peer(j)))

    def step4(u):
        s, h = UNITS[u]
        for copy in stage4[u]:
            copy.wait_recv()
        piece_a = qc.at[s, :, rows_at(base_a[h], y, 128)]
        piece_b = qc.at[s, :, rows_at(base_b[h], z, 128)]
        for j in (1, 2, 3):
            stage5[u].append(remote(piece_a, piece_a, y_peer(j)))
            stage5[u].append(remote(piece_b, piece_b, z_peer(j)))

    def step5(u):
        for copy in stage5[u]:
            copy.wait_recv()

    tile = jnp.full((RB, RB), K, jnp.int32)
    for k in range(K):
        tile = jnp.where(lcols[k : k + 1, :] == sub, k, tile)
    vtable[0:RB, 0:RB] = tile
    for s in range(2):
        tile = jnp.full((RB, RB), K if s else KS, jnp.int32)
        for k in range(KS):
            tile = jnp.where(scols[k][s : s + 1, :] == sub, k, tile)
        vtable[RB * (s + 1) : RB * (s + 2), 0:RB] = tile
    to_scalar = pltpu.make_async_copy(vtable, table, load_sem.at[4])
    to_scalar.start()

    def clear(i, _):
        aloc[i, K] = jnp.zeros((T, T), BF)
        asec[i, KS] = jnp.zeros((T, T), BF)
        return 0

    lax.fori_loop(0, RB, clear, 0, unroll=4)

    side_of = (lax.broadcasted_iota(jnp.int32, (16, 128), 1) >= T).astype(F32)
    slots = [(side_of + 2.0 * p).astype(BF) for p in range(4)]

    def spread_row(k, src, cols, dst, h):
        row = jnp.broadcast_to(cols(k), (16, 128))
        swapped = jnp.concatenate([row[:, T:], row[:, :T]], axis=1).astype(BF)
        row = row.astype(BF)
        masks = [(row == slots[p], swapped == slots[p]) for p in range(4)]
        for q in range(4):
            rows = pl.ds(pl.multiple_of(k * T + q * 16, 16), 16)
            t = src(rows)
            u = jnp.concatenate([t[:, T:], t[:, :T]], axis=1)
            for p in range(4):
                dst[rows, h * HALF + p * 128 : h * HALF + (p + 1) * 128] = jnp.where(
                    masks[p][0], t, jnp.where(masks[p][1], u, jnp.zeros_like(t))
                )

    def spread(start, stop, src, cols, dst, h):
        def body(k, _):
            spread_row(k, src, cols, dst, h)
            return 0

        lax.fori_loop(start, stop, body, 0, unroll=8)

    def fill(src, which, m, dst, pairs):
        for b in range(4):
            i = m * 4 + b
            for n, p in enumerate(pairs):
                dst[b * T : (b + 1) * T, n * 128 : (n + 1) * 128] = jnp.concatenate(
                    [src[i, table[which * RB + 2 * p, i]], src[i, table[which * RB + 2 * p + 1, i]]], axis=1
                )

    def rows_of(m):
        return pl.ds(pl.multiple_of(m * MT, MT), MT)

    def multiply(src, which, pairs, use, points=(), beside=None):
        fill(src, which, 0, ab0, pairs)

        def run(start, stop, extra):
            def body(jj, _):
                m = 2 * jj
                fill(src, which, m + 1, ab1, pairs)
                use(m, ab0)
                if extra is not None:
                    extra(jj - 2)
                fill(src, which, jnp.minimum(m + 2, 7), ab0, pairs)
                use(m + 1, ab1)
                return 0

            if stop > start:
                lax.fori_loop(start, stop, body, 0)

        at = 0
        for stop, point in points:
            run(at, stop, beside if at >= 2 else None)
            point()
            at = stop
        run(at, 4, beside if at >= 2 else None)

    def block(ab, depth, cols, dst, top):
        return jnp.dot(ab[:, :depth], dst[top : top + depth, cols], preferred_element_type=F32)

    def steps(*calls):
        def point():
            for step, arg in calls:
                step(arg)

        return point

    spread(0, RB, lambda rows: pc[rows, :], lambda k: mown[pl.ds(k, 1), :], d0, 0)
    to_scalar.wait()
    load_l.wait()

    def pass1(m, ab):
        for n in range(2):
            cols = slice(n * 256, (n + 1) * 256)
            acc[rows_of(m), cols] = block(ab, ROWS, cols, d0, 0)

    def rest(_):
        partner.append([remote(pc.at[halves[1]], pp.at[halves[1]], x_peer(2))])

    multiply(
        aloc, 0, range(16), pass1,
        [(1, steps((step1, 0))), (2, steps((step1, 1))), (3, steps((step2, 0), (rest, 0)))],
    )
    step2(1)

    def pass2(h):
        def use(m, ab):
            for n in range(2, 4):
                cols = slice(n * 256, (n + 1) * 256)
                part = block(ab, DEPTH, cols, d0, h * DEPTH)
                if h:
                    part += acc[rows_of(m), cols]
                acc[rows_of(m), cols] = part

        return use

    def begin(h):
        for copy in partner[h]:
            copy.wait_recv()
        if h == 0:
            mpart[...] = mp[...].astype(F32)
        spread(h * 16, h * 16 + 16, lambda rows: pp[rows, :], lambda k: mpart[pl.ds(k, 1), :], d0, 1)

    begin(0)
    multiply(aloc, 0, range(8), pass2(0), [(1, steps((step3, 0))), (3, steps((step3, 1), (step2, 2)))])
    step4(0)
    step2(3)
    begin(1)
    multiply(
        aloc, 0, range(8, 16), pass2(1), [(1, steps((step4, 1), (step3, 2))), (3, steps((step3, 3), (step4, 2)))]
    )
    load_s[1].start()
    load_s[0].wait()

    dense = [d1, d1, d0, d0]

    def spread_unit(u, k, h):
        s, half = UNITS[u]
        spread_row(
            half * 16 + k, lambda rows: qc[s, sides[h], rows, :], lambda k: mq[s, sides[h], pl.ds(k, 1), :], dense[u], h
        )

    def ahead(u):
        def extra(part):
            for k in range(8):
                for h in range(2):
                    spread_unit(u, part * 8 + k, h)

        return extra

    def place(m, h):
        return rows_of(m), pl.ds(pl.multiple_of((sides[h] * 2 + core) * HALF, HALF), HALF)

    def result(m, h):
        ref = out.at[place(m, h)]
        return pltpu.make_async_remote_copy(
            src_ref=ref, dst_ref=ref, send_sem=osend.at[m, h], recv_sem=orecv.at[m, h],
            device_id=core_peer, device_id_type=MESH,
        )

    def pass3(u):
        top = UNITS[u][1] * DEPTH

        def use(m, ab):
            for n in range(4):
                cols = slice(n * 256, (n + 1) * 256)
                acc[rows_of(m), cols] += block(ab, DEPTH, cols, dense[u], top)

        def last(m, ab):
            for h in range(2):
                cols = slice(h * HALF, (h + 1) * HALF)
                total = acc[rows_of(m), cols] + block(ab, DEPTH, cols, dense[u], top)
                out[place(m, h)] = total.astype(BF)
                result(m, h).start()

        return last if u == 3 else use

    step5(0)
    step4(3)
    for h in range(2):
        s, half = UNITS[0]
        spread(
            0, 16, lambda rows: qc[0, sides[h], rows, :], lambda k: mq[0, sides[h], pl.ds(k, 1), :], d1, h
        )
    for u, (s, half) in enumerate(UNITS):
        if u == 2:
            load_s[1].wait()
        more = u < 3
        multiply(
            aloc if s else asec, s + 1, range(half * 8, half * 8 + 8), pass3(u),
            [(2, steps((step5, u + 1)))] if more else (), ahead(u + 1) if more else None,
        )

    def finish(m, _):
        for h in range(2):
            result(m, h).wait()
        return 0

    lax.fori_loop(0, 8, finish, 0)
    for copy in sent:
        copy.wait_send()


def per_device(local_tiles, local_cols, section_tiles, section_cols, owners, prol_tiles, prol_cols):
    vmem = pl.BlockSpec(memory_space=pltpu.VMEM)
    smem = pl.BlockSpec(memory_space=pltpu.SMEM)
    hbm = pl.BlockSpec(memory_space=pl.ANY)

    def b(*shape):
        return pltpu.VMEM(shape, BF)

    def f(*shape):
        return pltpu.VMEM(shape, F32)

    return pl.pallas_call(
        kernel,
        out_shape=pltpu.VMEM((ROWS, 2048), BF),
        in_specs=[vmem, vmem, vmem, smem, hbm, hbm, hbm],
        out_specs=vmem,
        scratch_shapes=[
            b(RB, 2, T, T), b(RB, K + 1, T, T), b(RB, KS + 1, T, T), b(ROWS, 128), b(ROWS, 128),
            b(RB, 128), b(RB, 128), f(RB, 128), f(RB, 128), f(2, 2, RB, 128),
            b(4, 128, 128), b(4, 128, 128), b(4, 128, 128), b(4, 128, 128),
            b(4, RB, 128), b(4, 2, 128, 128), b(2, RB, 128),
            *[b(2, 4, 32, 128) for _ in UNITS], b(4, RB, 128), b(4, RB, 128),
            b(4, 2, 32, 128), b(2, RB, 128),
            *[b(4, 2, 32, 128) for _ in UNITS], b(4, RB, 128), b(4, RB, 128),
            b(2, 2, ROWS, 128), b(ROWS, WIDE), b(ROWS, WIDE), b(MT, ROWS), b(MT, ROWS), f(ROWS, WIDE),
            pltpu.VMEM((3 * RB, 128), jnp.int32), pltpu.SMEM((3 * RB, 128), jnp.int32),
            pltpu.SemaphoreType.DMA((5,)),
            pltpu.SemaphoreType.DMA((COPIES,)), pltpu.SemaphoreType.DMA((COPIES,)),
            pltpu.SemaphoreType.DMA((8, 2)), pltpu.SemaphoreType.DMA((8, 2)),
        ],
        compiler_params=pltpu.CompilerParams(
            collective_id=0, has_side_effects=True, vmem_limit_bytes=46 * 2**20
        ),
        name="galerkin",
    )(local_cols.T, section_cols.transpose(2, 1, 0), prol_cols.T, owners, prol_tiles, local_tiles, section_tiles)


def solution(mesh):
    in_specs = (
        P("rows", None, None, None),
        P("rows", None),
        P("rows", None, None, None, None),
        P("rows", None, None),
        P(),
        P("rows", "cols", None, None),
        P("rows", "cols"),
    )
    return jax.shard_map(
        per_device, mesh=mesh, in_specs=in_specs, out_specs=P("rows", None), check_vma=False
    )
```

```python
import jax
import jax.numpy as jnp
from jax import lax
from jax.experimental import pallas as pl
from jax.experimental.pallas import tpu as pltpu
from jax.sharding import PartitionSpec as P

MESH = pl.DeviceIdType.MESH
BF = jnp.bfloat16
F32 = jnp.float32
T = 64
RB = 32
K = 24
KS = 12
MT = 256
ROWS = RB * T
DEPTH = ROWS // 2
HALF = 512
WIDE = 2 * HALF
UNITS = [(0, 0), (0, 1), (1, 0), (1, 1)]
COPIES = 128


def kernel(lcols, scols, pcols, owners, p_hbm, l_hbm, s_hbm, out, *scratch):
    refs = iter(scratch)

    def take(n):
        return [next(refs) for _ in range(n)]

    praw, aloc, asec, pc, pp, meta, mp, mown, mpart, mq = take(10)
    r1a, r1b = take(2), take(2)
    r1m, s1, s1m = take(3)
    r2, r2m = take(4), take(2)
    s2, s2m = take(2)
    rx, rxm = take(4), take(2)
    qc, d0, d1, ab0, ab1, acc, vtable, table = take(8)
    load_sem, send_sem, recv_sem, osend, orecv = take(5)

    r = lax.axis_index("rows")
    c = lax.axis_index("cols")
    y, xl, z = r // 8, (r // 4) % 2, r % 4
    xh, core = c // 2, c % 2
    x = xh * 2 + xl
    sides = [xh, 1 - xh]

    def y_peer(j):
        return (((y + j) % 4 * 2 + xl) * 4 + z, c)

    def z_peer(j):
        return ((y * 2 + xl) * 4 + (z + j) % 4, c)

    def x_peer(j):
        q = (x + j) % 4
        return ((y * 2 + q % 2) * 4 + z, (q // 2) * 2 + core)

    core_peer = (r, xh * 2 + 1 - core)

    load_p = pltpu.make_async_copy(p_hbm, praw, load_sem.at[0])
    load_l = [
        pltpu.make_async_copy(
            l_hbm.at[pl.ds(8 * i, 8)], aloc.at[pl.ds(8 * i, 8), pl.ds(0, K)], load_sem.at[4 + i]
        )
        for i in range(4)
    ]
    load_s = [
        pltpu.make_async_copy(s_hbm.at[:, 0], asec.at[:, pl.ds(0, KS)], load_sem.at[2]),
        pltpu.make_async_copy(s_hbm.at[:, 1], aloc.at[:, pl.ds(0, KS)], load_sem.at[3]),
    ]
    load_p.start()
    for load in load_l:
        load.start()

    barrier = pltpu.get_barrier_semaphore()
    for peer in [f(j) for f in (y_peer, z_peer, x_peer) for j in (1, 2, 3)] + [core_peer]:
        pl.semaphore_signal(barrier, inc=1, device_id=peer, device_id_type=MESH)

    sub = lax.broadcasted_iota(jnp.int32, (RB, RB), 0)
    lane = lax.broadcasted_iota(jnp.int32, (RB, RB), 1)
    first, second = [
        jnp.sum(jnp.where(sub == lane, pcols[j : j + 1, :], 0).astype(F32), axis=1, keepdims=True) for j in range(2)
    ]
    mown[...] = jnp.where(lax.broadcasted_iota(jnp.int32, (RB, 128), 1) < T, first, second)
    meta[...] = mown[...].astype(BF)

    def owner(s):
        o = owners[s]
        return o // 8, (o // 4) % 2, o % 4

    sent = []

    def remote(src, dst, peer):
        i = len(sent)
        copy = pltpu.make_async_remote_copy(
            src_ref=src, dst_ref=dst, send_sem=send_sem.at[i], recv_sem=recv_sem.at[i],
            device_id=peer, device_id_type=MESH,
        )
        copy.start()
        sent.append(copy)
        return copy

    def rows_at(base, index, size):
        return pl.ds(pl.multiple_of(base + index * size, size), size)

    load_p.wait()

    def compact(k, _):
        rows = pl.ds(pl.multiple_of(k * T, T), T)
        pc[rows, :] = jnp.concatenate([praw[k, 0], praw[k, 1]], axis=1)
        return 0

    lax.fori_loop(0, RB, compact, 0, unroll=4)
    pl.semaphore_wait(barrier, 10)

    base_a = [u * DEPTH for u in range(2)]
    base_b = [u * DEPTH + DEPTH // 2 for u in range(2)]
    stage1 = [[], []]
    for h in range(2):
        for j in (1, 2, 3):
            stage1[h].append(remote(pc.at[rows_at(base_a[h], (y + j) % 4, 128)], r1a[h].at[j], y_peer(j)))
            stage1[h].append(remote(pc.at[rows_at(base_b[h], (z + j) % 4, 128)], r1b[h].at[j], z_peer(j)))
            if h == 0:
                stage1[h].append(remote(meta, r1m.at[j], y_peer(j)))
    halves = [pl.ds(0, DEPTH), pl.ds(DEPTH, DEPTH)]
    partner = [[remote(meta, mp, x_peer(2)), remote(pc.at[halves[0]], pp.at[halves[0]], x_peer(2))]]
    for h in range(2):
        r1a[h][0] = pc[rows_at(base_a[h], y, 128)]
        r1b[h][0] = pc[rows_at(base_b[h], z, 128)]
    r1m[0] = meta[...]

    stage2, stage3, stage4, stage5 = [[[] for _ in UNITS] for _ in range(4)]

    def step1(h):
        for copy in stage1[h]:
            copy.wait_recv()
        for s in range(2):
            u = 2 * s + h
            oy, ox, oz = owner(s)
            s1[u, 0] = r1a[h][(y + 4 - oy) % 4]
            s1[u, 1] = r1b[h][(z + 4 - oz) % 4]
            if h == 0:
                s1m[s] = r1m[(y + 4 - oy) % 4]
            for j in (1, 2, 3):
                stage2[u].append(remote(s1.at[u, 0, rows_at(0, (z + j) % 4, 32)], r2[u].at[0, j], z_peer(j)))
                stage2[u].append(remote(s1.at[u, 1, rows_at(0, (y + j) % 4, 32)], r2[u].at[1, j], y_peer(j)))
                if h == 0:
                    stage2[u].append(remote(s1m.at[s], r2m[s].at[j], z_peer(j)))
            r2[u][0, 0] = s1[u, 0, rows_at(0, z, 32)]
            r2[u][1, 0] = s1[u, 1, rows_at(0, y, 32)]
            if h == 0:
                r2m[s][0] = s1m[s]

    def step2(u):
        s, h = UNITS[u]
        for copy in stage2[u]:
            copy.wait_recv()
        oy, ox, oz = owner(s)
        s2[u, 0] = r2[u][0, (z + 4 - oz) % 4]
        s2[u, 1] = r2[u][1, (y + 4 - oy) % 4]
        for j in (1, 2, 3):
            stage3[u].append(remote(s2.at[u], rx[u].at[j], x_peer(j)))
        rx[u][0] = s2[u]
        if h == 0:
            s2m[s] = r2m[s][(z + 4 - oz) % 4]
            for j in (1, 2, 3):
                stage3[u].append(remote(s2m.at[s], rxm[s].at[j], x_peer(j)))
            rxm[s][0] = s2m[s]

    def step3(u):
        s, h = UNITS[u]
        for copy in stage3[u]:
            copy.wait_recv()
        oy, ox, oz = owner(s)
        mine_a = rows_at(base_a[h], y * 4 + z, 32)
        mine_b = rows_at(base_b[h], z * 4 + y, 32)
        for side in range(2):
            slot = (x + 4 - (side * 2 + ox)) % 4
            qc[s, side, mine_a] = rx[u][slot, 0]
            qc[s, side, mine_b] = rx[u][slot, 1]
            if h == 0:
                mq[s, side] = rxm[s][slot].astype(F32)
        piece_a, piece_b = qc.at[s, :, mine_a], qc.at[s, :, mine_b]
        for j in (1, 2, 3):
            stage4[u].append(remote(piece_a, piece_a, z_peer(j)))
            stage4[u].append(remote(piece_b, piece_b, y_peer(j)))

    def step4(u):
        s, h = UNITS[u]
        for copy in stage4[u]:
            copy.wait_recv()
        piece_a = qc.at[s, :, rows_at(base_a[h], y, 128)]
        piece_b = qc.at[s, :, rows_at(base_b[h], z, 128)]
        for j in (1, 2, 3):
            stage5[u].append(remote(piece_a, piece_a, y_peer(j)))
            stage5[u].append(remote(piece_b, piece_b, z_peer(j)))

    def step5(u):
        for copy in stage5[u]:
            copy.wait_recv()

    tile = jnp.full((RB, RB), K, jnp.int32)
    for k in range(K):
        tile = jnp.where(lcols[k : k + 1, :] == sub, k, tile)
    vtable[0:RB, 0:RB] = tile
    for s in range(2):
        tile = jnp.full((RB, RB), K if s else KS, jnp.int32)
        for k in range(KS):
            tile = jnp.where(scols[k][s : s + 1, :] == sub, k, tile)
        vtable[RB * (s + 1) : RB * (s + 2), 0:RB] = tile
    to_scalar = pltpu.make_async_copy(vtable, table, load_sem.at[1])
    to_scalar.start()

    def clear(i, _):
        aloc[i, K] = jnp.zeros((T, T), BF)
        asec[i, KS] = jnp.zeros((T, T), BF)
        return 0

    lax.fori_loop(0, RB, clear, 0, unroll=4)

    side_of = (lax.broadcasted_iota(jnp.int32, (16, 128), 1) >= T).astype(F32)
    slots = [(side_of + 2.0 * p).astype(BF) for p in range(4)]

    def spread_row(k, src, cols, dst, h):
        row = jnp.broadcast_to(cols(k), (16, 128))
        swapped = jnp.concatenate([row[:, T:], row[:, :T]], axis=1).astype(BF)
        row = row.astype(BF)
        masks = [(row == slots[p], swapped == slots[p]) for p in range(4)]
        for q in range(4):
            rows = pl.ds(pl.multiple_of(k * T + q * 16, 16), 16)
            t = src(rows)
            u = jnp.concatenate([t[:, T:], t[:, :T]], axis=1)
            for p in range(4):
                dst[rows, h * HALF + p * 128 : h * HALF + (p + 1) * 128] = jnp.where(
                    masks[p][0], t, jnp.where(masks[p][1], u, jnp.zeros_like(t))
                )

    def spread(start, stop, src, cols, dst, h):
        def body(k, _):
            spread_row(k, src, cols, dst, h)
            return 0

        lax.fori_loop(start, stop, body, 0, unroll=8)

    def fill(src, which, m, dst, pairs):
        for b in range(4):
            i = m * 4 + b
            for n, p in enumerate(pairs):
                dst[b * T : (b + 1) * T, n * 128 : (n + 1) * 128] = jnp.concatenate(
                    [src[i, table[which * RB + 2 * p, i]], src[i, table[which * RB + 2 * p + 1, i]]], axis=1
                )

    def rows_of(m):
        return pl.ds(pl.multiple_of(m * MT, MT), MT)

    def multiply(src, which, pairs, use, points=(), beside=None):
        fill(src, which, 0, ab0, pairs)

        def run(start, stop, extra):
            def body(jj, _):
                m = 2 * jj
                fill(src, which, m + 1, ab1, pairs)
                use(m, ab0)
                if extra is not None:
                    extra(jj - 2)
                fill(src, which, jnp.minimum(m + 2, 7), ab0, pairs)
                use(m + 1, ab1)
                return 0

            if stop > start:
                lax.fori_loop(start, stop, body, 0)

        at = 0
        for stop, point in points:
            run(at, stop, beside if at >= 2 else None)
            point()
            at = stop
        run(at, 4, beside if at >= 2 else None)

    def block(ab, depth, cols, dst, top):
        return jnp.dot(ab[:, :depth], dst[top : top + depth, cols], preferred_element_type=F32)

    def steps(*calls):
        def point():
            for step, arg in calls:
                step(arg)

        return point

    spread(0, RB, lambda rows: pc[rows, :], lambda k: mown[pl.ds(k, 1), :], d0, 0)
    to_scalar.wait()
    for load in load_l:
        load.wait()
    load_s[0].start()

    def pass1(m, ab):
        for n in range(2):
            cols = slice(n * 256, (n + 1) * 256)
            acc[rows_of(m), cols] = block(ab, ROWS, cols, d0, 0)

    def rest(_):
        partner.append([remote(pc.at[halves[1]], pp.at[halves[1]], x_peer(2))])

    multiply(
        aloc, 0, range(16), pass1,
        [(1, steps((step1, 0), (rest, 0))), (2, steps((step1, 1))), (3, steps((step2, 0)))],
    )
    step2(1)

    def pass2(h):
        def use(m, ab):
            for n in range(2, 4):
                cols = slice(n * 256, (n + 1) * 256)
                part = block(ab, DEPTH, cols, d0, h * DEPTH)
                if h:
                    part += acc[rows_of(m), cols]
                acc[rows_of(m), cols] = part

        return use

    def begin(h):
        for copy in partner[h]:
            copy.wait_recv()
        if h == 0:
            mpart[...] = mp[...].astype(F32)
        spread(h * 16, h * 16 + 16, lambda rows: pp[rows, :], lambda k: mpart[pl.ds(k, 1), :], d0, 1)

    begin(0)
    multiply(aloc, 0, range(8), pass2(0), [(1, steps((step3, 0))), (3, steps((step3, 1), (step2, 2)))])
    step4(0)
    step2(3)
    begin(1)
    multiply(
        aloc, 0, range(8, 16), pass2(1), [(1, steps((step4, 1))), (3, steps((step3, 2)))]
    )
    step3(3)
    load_s[1].start()
    load_s[0].wait()

    dense = [d1, d1, d0, d0]

    def spread_unit(u, k, h):
        s, half = UNITS[u]
        spread_row(
            half * 16 + k, lambda rows: qc[s, sides[h], rows, :], lambda k: mq[s, sides[h], pl.ds(k, 1), :], dense[u], h
        )

    def ahead(u):
        def extra(part):
            for k in range(8):
                for h in range(2):
                    spread_unit(u, part * 8 + k, h)

        return extra

    def place(m, h):
        return rows_of(m), pl.ds(pl.multiple_of((sides[h] * 2 + core) * HALF, HALF), HALF)

    def result(m, h):
        ref = out.at[place(m, h)]
        return pltpu.make_async_remote_copy(
            src_ref=ref, dst_ref=ref, send_sem=osend.at[m, h], recv_sem=orecv.at[m, h],
            device_id=core_peer, device_id_type=MESH,
        )

    def pass3(u):
        def use(m, ab):
            for n in range(4):
                cols = slice(n * 256, (n + 1) * 256)
                acc[rows_of(m), cols] += block(ab, DEPTH, cols, d1, u * DEPTH)

        return use

    def last(m, ab):
        for h in range(2):
            cols = slice(h * HALF, (h + 1) * HALF)
            total = acc[rows_of(m), cols] + block(ab, ROWS, cols, d0, 0)
            out[place(m, h)] = total.astype(BF)
            result(m, h).start()

    def spread_all(u):
        s, half = UNITS[u]
        for h in range(2):
            spread(
                half * 16, half * 16 + 16, lambda rows: qc[s, sides[h], rows, :],
                lambda k: mq[s, sides[h], pl.ds(k, 1), :], dense[u], h,
            )

    step5(0)
    spread_all(0)
    multiply(asec, 1, range(8), pass3(0), [(2, steps((step5, 1), (step4, 2)))], ahead(1))
    step4(3)
    multiply(asec, 1, range(8, 16), pass3(1), [(2, steps((step5, 2)))], ahead(2))
    load_s[1].wait()
    step5(3)
    spread_all(3)
    multiply(aloc, 2, range(16), last)

    def finish(m, _):
        for h in range(2):
            result(m, h).wait()
        return 0

    lax.fori_loop(0, 8, finish, 0)
    for copy in sent:
        copy.wait_send()


def per_device(local_tiles, local_cols, section_tiles, section_cols, owners, prol_tiles, prol_cols):
    vmem = pl.BlockSpec(memory_space=pltpu.VMEM)
    smem = pl.BlockSpec(memory_space=pltpu.SMEM)
    hbm = pl.BlockSpec(memory_space=pl.ANY)

    def b(*shape):
        return pltpu.VMEM(shape, BF)

    def f(*shape):
        return pltpu.VMEM(shape, F32)

    return pl.pallas_call(
        kernel,
        out_shape=pltpu.VMEM((ROWS, 2048), BF),
        in_specs=[vmem, vmem, vmem, smem, hbm, hbm, hbm],
        out_specs=vmem,
        scratch_shapes=[
            b(RB, 2, T, T), b(RB, K + 1, T, T), b(RB, KS + 1, T, T), b(ROWS, 128), b(ROWS, 128),
            b(RB, 128), b(RB, 128), f(RB, 128), f(RB, 128), f(2, 2, RB, 128),
            b(4, 128, 128), b(4, 128, 128), b(4, 128, 128), b(4, 128, 128),
            b(4, RB, 128), b(4, 2, 128, 128), b(2, RB, 128),
            *[b(2, 4, 32, 128) for _ in UNITS], b(4, RB, 128), b(4, RB, 128),
            b(4, 2, 32, 128), b(2, RB, 128),
            *[b(4, 2, 32, 128) for _ in UNITS], b(4, RB, 128), b(4, RB, 128),
            b(2, 2, ROWS, 128), b(ROWS, WIDE), b(ROWS, WIDE), b(MT, ROWS), b(MT, ROWS), f(ROWS, WIDE),
            pltpu.VMEM((3 * RB, 128), jnp.int32), pltpu.SMEM((3 * RB, 128), jnp.int32),
            pltpu.SemaphoreType.DMA((8,)),
            pltpu.SemaphoreType.DMA((COPIES,)), pltpu.SemaphoreType.DMA((COPIES,)),
            pltpu.SemaphoreType.DMA((8, 2)), pltpu.SemaphoreType.DMA((8, 2)),
        ],
        compiler_params=pltpu.CompilerParams(
            collective_id=0, has_side_effects=True, vmem_limit_bytes=46 * 2**20
        ),
        name="galerkin",
    )(local_cols.T, section_cols.transpose(2, 1, 0), prol_cols.T, owners, prol_tiles, local_tiles, section_tiles)


def solution(mesh):
    in_specs = (
        P("rows", None, None, None),
        P("rows", None),
        P("rows", None, None, None, None),
        P("rows", None, None),
        P(),
        P("rows", "cols", None, None),
        P("rows", "cols"),
    )
    return jax.shard_map(
        per_device, mesh=mesh, in_specs=in_specs, out_specs=P("rows", None), check_vma=False
    )
```

```python
import jax
import jax.numpy as jnp
from jax import lax
from jax.experimental import pallas as pl
from jax.experimental.pallas import tpu as pltpu
from jax.sharding import PartitionSpec as P

MESH = pl.DeviceIdType.MESH
BF = jnp.bfloat16
F32 = jnp.float32
T = 64
RB = 32
K = 24
KS = 12
MT = 256
ROWS = RB * T
DEPTH = ROWS // 2
HALF = 512
WIDE = 2 * HALF
UNITS = [(0, 0), (0, 1), (1, 0), (1, 1)]
COPIES = 128


def kernel(lcols, scols, pcols, owners, p_hbm, l_hbm, s_hbm, out, *scratch):
    refs = iter(scratch)

    def take(n):
        return [next(refs) for _ in range(n)]

    praw, aloc, asec, pc, pp, meta, mp, mown, mpart, mq = take(10)
    r1a, r1b = take(2), take(2)
    r1m, s1, s1m = take(3)
    r2, r2m = take(4), take(2)
    s2, s2m = take(2)
    rx, rxm = take(4), take(2)
    qc, d0, d1, ab0, ab1, acc, vtable, table = take(8)
    load_sem, send_sem, recv_sem, osend, orecv = take(5)

    r = lax.axis_index("rows")
    c = lax.axis_index("cols")
    y, xl, z = r // 8, (r // 4) % 2, r % 4
    xh, core = c // 2, c % 2
    x = xh * 2 + xl
    sides = [xh, 1 - xh]

    def y_peer(j):
        return (((y + j) % 4 * 2 + xl) * 4 + z, c)

    def z_peer(j):
        return ((y * 2 + xl) * 4 + (z + j) % 4, c)

    def x_peer(j):
        q = (x + j) % 4
        return ((y * 2 + q % 2) * 4 + z, (q // 2) * 2 + core)

    core_peer = (r, xh * 2 + 1 - core)

    load_p = pltpu.make_async_copy(p_hbm, praw, load_sem.at[0])
    load_l = [
        pltpu.make_async_copy(
            l_hbm.at[pl.ds(8 * i, 8)], aloc.at[pl.ds(8 * i, 8), pl.ds(0, K)], load_sem.at[4 + i]
        )
        for i in range(4)
    ]
    load_s = [
        pltpu.make_async_copy(s_hbm.at[:, 0], asec.at[:, pl.ds(0, KS)], load_sem.at[2]),
        pltpu.make_async_copy(s_hbm.at[:, 1], aloc.at[:, pl.ds(0, KS)], load_sem.at[3]),
    ]
    load_p.start()
    for load in load_l:
        load.start()

    barrier = pltpu.get_barrier_semaphore()
    for peer in [f(j) for f in (y_peer, z_peer, x_peer) for j in (1, 2, 3)] + [core_peer]:
        pl.semaphore_signal(barrier, inc=1, device_id=peer, device_id_type=MESH)

    sub = lax.broadcasted_iota(jnp.int32, (RB, RB), 0)
    lane = lax.broadcasted_iota(jnp.int32, (RB, RB), 1)
    first, second = [
        jnp.sum(jnp.where(sub == lane, pcols[j : j + 1, :], 0).astype(F32), axis=1, keepdims=True) for j in range(2)
    ]
    mown[...] = jnp.where(lax.broadcasted_iota(jnp.int32, (RB, 128), 1) < T, first, second)
    meta[...] = mown[...].astype(BF)

    def owner(s):
        o = owners[s]
        return o // 8, (o // 4) % 2, o % 4

    sent = []

    def remote(src, dst, peer):
        i = len(sent)
        copy = pltpu.make_async_remote_copy(
            src_ref=src, dst_ref=dst, send_sem=send_sem.at[i], recv_sem=recv_sem.at[i],
            device_id=peer, device_id_type=MESH,
        )
        copy.start()
        sent.append(copy)
        return copy

    def rows_at(base, index, size):
        return pl.ds(pl.multiple_of(base + index * size, size), size)

    tile = jnp.full((RB, RB), K, jnp.int32)
    for k in range(K):
        tile = jnp.where(lcols[k : k + 1, :] == sub, k, tile)
    vtable[0:RB, 0:RB] = tile
    for s in range(2):
        tile = jnp.full((RB, RB), K if s else KS, jnp.int32)
        for k in range(KS):
            tile = jnp.where(scols[k][s : s + 1, :] == sub, k, tile)
        vtable[RB * (s + 1) : RB * (s + 2), 0:RB] = tile
    to_scalar = pltpu.make_async_copy(vtable, table, load_sem.at[1])
    to_scalar.start()

    def clear(i, _):
        aloc[i, K] = jnp.zeros((T, T), BF)
        asec[i, KS] = jnp.zeros((T, T), BF)
        return 0

    lax.fori_loop(0, RB, clear, 0, unroll=4)

    load_p.wait()

    def compact(k, _):
        rows = pl.ds(pl.multiple_of(k * T, T), T)
        pc[rows, :] = jnp.concatenate([praw[k, 0], praw[k, 1]], axis=1)
        return 0

    lax.fori_loop(0, RB, compact, 0, unroll=4)
    pl.semaphore_wait(barrier, 10)

    base_a = [u * DEPTH for u in range(2)]
    base_b = [u * DEPTH + DEPTH // 2 for u in range(2)]
    stage1 = [[], []]
    for h in range(2):
        for j in (1, 2, 3):
            stage1[h].append(remote(pc.at[rows_at(base_a[h], (y + j) % 4, 128)], r1a[h].at[j], y_peer(j)))
            stage1[h].append(remote(pc.at[rows_at(base_b[h], (z + j) % 4, 128)], r1b[h].at[j], z_peer(j)))
            if h == 0:
                stage1[h].append(remote(meta, r1m.at[j], y_peer(j)))
    halves = [pl.ds(0, DEPTH), pl.ds(DEPTH, DEPTH)]
    partner = [[remote(meta, mp, x_peer(2)), remote(pc.at[halves[0]], pp.at[halves[0]], x_peer(2))]]
    for h in range(2):
        r1a[h][0] = pc[rows_at(base_a[h], y, 128)]
        r1b[h][0] = pc[rows_at(base_b[h], z, 128)]
    r1m[0] = meta[...]

    stage2, stage3, stage4, stage5 = [[[] for _ in UNITS] for _ in range(4)]

    def step1(h):
        for copy in stage1[h]:
            copy.wait_recv()
        for s in range(2):
            u = 2 * s + h
            oy, ox, oz = owner(s)
            s1[u, 0] = r1a[h][(y + 4 - oy) % 4]
            s1[u, 1] = r1b[h][(z + 4 - oz) % 4]
            if h == 0:
                s1m[s] = r1m[(y + 4 - oy) % 4]
            for j in (1, 2, 3):
                stage2[u].append(remote(s1.at[u, 0, rows_at(0, (z + j) % 4, 32)], r2[u].at[0, j], z_peer(j)))
                stage2[u].append(remote(s1.at[u, 1, rows_at(0, (y + j) % 4, 32)], r2[u].at[1, j], y_peer(j)))
                if h == 0:
                    stage2[u].append(remote(s1m.at[s], r2m[s].at[j], z_peer(j)))
            r2[u][0, 0] = s1[u, 0, rows_at(0, z, 32)]
            r2[u][1, 0] = s1[u, 1, rows_at(0, y, 32)]
            if h == 0:
                r2m[s][0] = s1m[s]

    def step2(u):
        s, h = UNITS[u]
        for copy in stage2[u]:
            copy.wait_recv()
        oy, ox, oz = owner(s)
        s2[u, 0] = r2[u][0, (z + 4 - oz) % 4]
        s2[u, 1] = r2[u][1, (y + 4 - oy) % 4]
        for j in (1, 2, 3):
            stage3[u].append(remote(s2.at[u], rx[u].at[j], x_peer(j)))
        rx[u][0] = s2[u]
        if h == 0:
            s2m[s] = r2m[s][(z + 4 - oz) % 4]
            for j in (1, 2, 3):
                stage3[u].append(remote(s2m.at[s], rxm[s].at[j], x_peer(j)))
            rxm[s][0] = s2m[s]

    def step3(u):
        s, h = UNITS[u]
        for copy in stage3[u]:
            copy.wait_recv()
        oy, ox, oz = owner(s)
        mine_a = rows_at(base_a[h], y * 4 + z, 32)
        mine_b = rows_at(base_b[h], z * 4 + y, 32)
        for side in range(2):
            slot = (x + 4 - (side * 2 + ox)) % 4
            qc[s, side, mine_a] = rx[u][slot, 0]
            qc[s, side, mine_b] = rx[u][slot, 1]
            if h == 0:
                mq[s, side] = rxm[s][slot].astype(F32)
        piece_a, piece_b = qc.at[s, :, mine_a], qc.at[s, :, mine_b]
        for j in (1, 2, 3):
            stage4[u].append(remote(piece_a, piece_a, z_peer(j)))
            stage4[u].append(remote(piece_b, piece_b, y_peer(j)))

    def step4(u):
        s, h = UNITS[u]
        for copy in stage4[u]:
            copy.wait_recv()
        piece_a = qc.at[s, :, rows_at(base_a[h], y, 128)]
        piece_b = qc.at[s, :, rows_at(base_b[h], z, 128)]
        for j in (1, 2, 3):
            stage5[u].append(remote(piece_a, piece_a, y_peer(j)))
            stage5[u].append(remote(piece_b, piece_b, z_peer(j)))

    def step5(u):
        for copy in stage5[u]:
            copy.wait_recv()

    side_of = (lax.broadcasted_iota(jnp.int32, (16, 128), 1) >= T).astype(F32)
    slots = [(side_of + 2.0 * p).astype(BF) for p in range(4)]

    def spread_row(k, src, cols, dst, h):
        row = jnp.broadcast_to(cols(k), (16, 128))
        swapped = jnp.concatenate([row[:, T:], row[:, :T]], axis=1).astype(BF)
        row = row.astype(BF)
        masks = [(row == slots[p], swapped == slots[p]) for p in range(4)]
        for q in range(4):
            rows = pl.ds(pl.multiple_of(k * T + q * 16, 16), 16)
            t = src(rows)
            u = jnp.concatenate([t[:, T:], t[:, :T]], axis=1)
            for p in range(4):
                dst[rows, h * HALF + p * 128 : h * HALF + (p + 1) * 128] = jnp.where(
                    masks[p][0], t, jnp.where(masks[p][1], u, jnp.zeros_like(t))
                )

    def spread(start, stop, src, cols, dst, h):
        def body(k, _):
            spread_row(k, src, cols, dst, h)
            return 0

        lax.fori_loop(start, stop, body, 0, unroll=8)

    def fill(src, which, m, dst, pairs):
        for b in range(4):
            i = m * 4 + b
            for n, p in enumerate(pairs):
                dst[b * T : (b + 1) * T, n * 128 : (n + 1) * 128] = jnp.concatenate(
                    [src[i, table[which * RB + 2 * p, i]], src[i, table[which * RB + 2 * p + 1, i]]], axis=1
                )

    def rows_of(m):
        return pl.ds(pl.multiple_of(m * MT, MT), MT)

    def multiply(src, which, pairs, use, points=(), beside=None):
        fill(src, which, 0, ab0, pairs)

        def run(start, stop, extra):
            def body(jj, _):
                m = 2 * jj
                fill(src, which, m + 1, ab1, pairs)
                use(m, ab0)
                if extra is not None:
                    extra(jj - 2)
                fill(src, which, jnp.minimum(m + 2, 7), ab0, pairs)
                use(m + 1, ab1)
                return 0

            if stop > start:
                lax.fori_loop(start, stop, body, 0)

        at = 0
        for stop, point in points:
            run(at, stop, beside if at >= 2 else None)
            point()
            at = stop
        run(at, 4, beside if at >= 2 else None)

    def block(ab, depth, cols, dst, top):
        return jnp.dot(ab[:, :depth], dst[top : top + depth, cols], preferred_element_type=F32)

    def steps(*calls):
        def point():
            for step, arg in calls:
                step(arg)

        return point

    spread(0, RB, lambda rows: pc[rows, :], lambda k: mown[pl.ds(k, 1), :], d0, 0)
    to_scalar.wait()
    for load in load_l:
        load.wait()
    load_s[0].start()

    def pass1(m, ab):
        for n in range(2):
            cols = slice(n * 256, (n + 1) * 256)
            acc[rows_of(m), cols] = block(ab, ROWS, cols, d0, 0)

    def rest(_):
        partner.append([remote(pc.at[halves[1]], pp.at[halves[1]], x_peer(2))])

    multiply(
        aloc, 0, range(16), pass1,
        [(1, steps((step1, 0))), (2, steps((step1, 1))), (3, steps((step2, 0), (step2, 2), (step2, 1), (step2, 3), (rest, 0)))],
    )
    def pass2(h):
        def use(m, ab):
            for n in range(2, 4):
                cols = slice(n * 256, (n + 1) * 256)
                part = block(ab, DEPTH, cols, d0, h * DEPTH)
                if h:
                    part += acc[rows_of(m), cols]
                acc[rows_of(m), cols] = part

        return use

    def begin(h):
        for copy in partner[h]:
            copy.wait_recv()
        if h == 0:
            mpart[...] = mp[...].astype(F32)
        spread(h * 16, h * 16 + 16, lambda rows: pp[rows, :], lambda k: mpart[pl.ds(k, 1), :], d0, 1)

    begin(0)
    multiply(aloc, 0, range(8), pass2(0), [(1, steps((step3, 0), (step3, 1))), (3, steps((step3, 2), (step3, 3)))])
    step4(0)
    step4(1)
    begin(1)
    multiply(
        aloc, 0, range(8, 16), pass2(1), [(2, steps((step4, 2)))]
    )
    step4(3)
    load_s[1].start()
    load_s[0].wait()

    dense = [d1, d1, d0, d0]

    def spread_unit(u, k, h):
        s, half = UNITS[u]
        spread_row(
            half * 16 + k, lambda rows: qc[s, sides[h], rows, :], lambda k: mq[s, sides[h], pl.ds(k, 1), :], dense[u], h
        )

    def ahead(u):
        def extra(part):
            for k in range(8):
                for h in range(2):
                    spread_unit(u, part * 8 + k, h)

        return extra

    def place(m, h):
        return rows_of(m), pl.ds(pl.multiple_of((sides[h] * 2 + core) * HALF, HALF), HALF)

    def result(m, h):
        ref = out.at[place(m, h)]
        return pltpu.make_async_remote_copy(
            src_ref=ref, dst_ref=ref, send_sem=osend.at[m, h], recv_sem=orecv.at[m, h],
            device_id=core_peer, device_id_type=MESH,
        )

    def pass3(u):
        def use(m, ab):
            for n in range(4):
                cols = slice(n * 256, (n + 1) * 256)
                acc[rows_of(m), cols] += block(ab, DEPTH, cols, d1, u * DEPTH)

        return use

    def last(m, ab):
        for n in range(4):
            cols = slice(n * 256, (n + 1) * 256)
            start = (sides[n // 2] * 2 + core) * HALF + n % 2 * 256
            total = acc[rows_of(m), cols] + block(ab, ROWS, cols, d0, 0)
            out[rows_of(m), pl.ds(pl.multiple_of(start, 256), 256)] = total.astype(BF)
            if n % 2:
                result(m, n // 2).start()

    def spread_all(u):
        s, half = UNITS[u]
        for h in range(2):
            spread(
                half * 16, half * 16 + 16, lambda rows: qc[s, sides[h], rows, :],
                lambda k: mq[s, sides[h], pl.ds(k, 1), :], dense[u], h,
            )

    step5(0)
    spread_all(0)
    multiply(asec, 1, range(8), pass3(0), [(2, steps((step5, 1)))], ahead(1))
    multiply(asec, 1, range(8, 16), pass3(1), [(2, steps((step5, 2)))], ahead(2))
    load_s[1].wait()
    step5(3)
    spread_all(3)
    multiply(aloc, 2, range(16), last)

    def finish(m, _):
        for h in range(2):
            result(m, h).wait()
        return 0

    lax.fori_loop(0, 8, finish, 0)
    for copy in sent:
        copy.wait_send()


def per_device(local_tiles, local_cols, section_tiles, section_cols, owners, prol_tiles, prol_cols):
    vmem = pl.BlockSpec(memory_space=pltpu.VMEM)
    smem = pl.BlockSpec(memory_space=pltpu.SMEM)
    hbm = pl.BlockSpec(memory_space=pl.ANY)

    def b(*shape):
        return pltpu.VMEM(shape, BF)

    def f(*shape):
        return pltpu.VMEM(shape, F32)

    return pl.pallas_call(
        kernel,
        out_shape=pltpu.VMEM((ROWS, 2048), BF),
        in_specs=[vmem, vmem, vmem, smem, hbm, hbm, hbm],
        out_specs=vmem,
        scratch_shapes=[
            b(RB, 2, T, T), b(RB, K + 1, T, T), b(RB, KS + 1, T, T), b(ROWS, 128), b(ROWS, 128),
            b(RB, 128), b(RB, 128), f(RB, 128), f(RB, 128), f(2, 2, RB, 128),
            b(4, 128, 128), b(4, 128, 128), b(4, 128, 128), b(4, 128, 128),
            b(4, RB, 128), b(4, 2, 128, 128), b(2, RB, 128),
            *[b(2, 4, 32, 128) for _ in UNITS], b(4, RB, 128), b(4, RB, 128),
            b(4, 2, 32, 128), b(2, RB, 128),
            *[b(4, 2, 32, 128) for _ in UNITS], b(4, RB, 128), b(4, RB, 128),
            b(2, 2, ROWS, 128), b(ROWS, WIDE), b(ROWS, WIDE), b(MT, ROWS), b(MT, ROWS), f(ROWS, WIDE),
            pltpu.VMEM((3 * RB, 128), jnp.int32), pltpu.SMEM((3 * RB, 128), jnp.int32),
            pltpu.SemaphoreType.DMA((8,)),
            pltpu.SemaphoreType.DMA((COPIES,)), pltpu.SemaphoreType.DMA((COPIES,)),
            pltpu.SemaphoreType.DMA((8, 2)), pltpu.SemaphoreType.DMA((8, 2)),
        ],
        compiler_params=pltpu.CompilerParams(
            collective_id=0, has_side_effects=True, vmem_limit_bytes=46 * 2**20
        ),
        name="galerkin",
    )(local_cols.T, section_cols.transpose(2, 1, 0), prol_cols.T, owners, prol_tiles, local_tiles, section_tiles)


def solution(mesh):
    in_specs = (
        P("rows", None, None, None),
        P("rows", None),
        P("rows", None, None, None, None),
        P("rows", None, None),
        P(),
        P("rows", "cols", None, None),
        P("rows", "cols"),
    )
    return jax.shard_map(
        per_device, mesh=mesh, in_specs=in_specs, out_specs=P("rows", None), check_vma=False
    )
```
